32 devices in a mesh: groups: 2 (over y), space: 4 (over z), member: 2 (over x), chan: 2 (over core).
Axes of the slice: x: 2, y: 2, z: 4, core: 2. Of those that a mesh axis runs over, the one named last changes fastest.
Arguments:
- mesh_state: bfloat16 [4, 96, 128, 256], P(('groups', 'member'), ('space', 'chan')), parts along dimension 0, may hold values from -6 to 6
- boundary: bfloat16 [4, 32, 128, 256], P(('groups', 'member'), 'space'), parts along dimension 0, may hold values from -6 to 6
- boundary_send: int32 [8, 4, 3], P('groups'), parts along dimension 0, may hold values from 0 to 7
- boundary_count: int32 [8, 4], P('groups'), parts along dimension 0, may hold values from 0 to 3, as said below
- grid_edges: int32 [192, 4], P(('groups', 'space', 'chan')), parts along dimension 0, may hold values from 0 to 11
- edge_tiles: int32 [16], P(('groups', 'space')), parts along dimension 0, may hold values from 0 to 23
- halo_source: int32 [64], P(('groups', 'space')), parts along dimension 0, may hold values from 0 to 7
- halo_count: int32 [8], P(('groups', 'space')), parts along dimension 0, may hold values from 1 to 8, as said below
- mesh_edges: int32 [192, 8], P(('groups', 'space', 'chan')), parts along dimension 0, may hold values from 0 to 31
- edge_first: bfloat16 [2, 2, 256, 256], replicated, may hold values from -0.25 to 0.25
- edge_bias: float32 [2, 256], replicated, may hold values from -3 to 3
- edge_second: bfloat16 [2, 256, 256], replicated, may hold values from -0.125 to 0.125
- node_first: bfloat16 [2, 2, 256, 256], replicated, may hold values from -0.25 to 0.25
- node_bias: float32 [2, 256], replicated, may hold values from -3 to 3
- node_second: bfloat16 [2, 256, 256], replicated, may hold values from -0.375 to 0.375
- node_gain: float32 [2, 256], replicated, may hold values from 0.1 to 1.9
Outputs:
- processed: bfloat16 [4, 96, 128, 256], P(('groups', 'member'), ('space', 'chan')), parts along dimension 0
The draws below stay inside these ranges and needn't reach their ends.
There are 2 independent parts, one for each index of `groups`. The reference program is written for one: setup_inputs(seed, part) draws one part's arguments, and reference() takes and returns one part's arrays. A program takes and returns all parts, laid end to end along the dimension named above; an argument that names none is the same for every part. Nothing has to cross between parts.
Inputs may be any that keep to these rules, and one draw needn't show every extreme that they name: `boundary_count`: 3 is reached by some pair. `halo_count`: 8 is reached by some partition.
All inputs are finite; a program needn't handle non-finite values.
Results may differ from the reference program's by a relative error of at most 0.0063.
Values may be sent and summed in bfloat16 or wider, within the bound.
A program may use at most 64 MiB of HBM per device.

```python
import jax
import jax.numpy as jnp
from jax import lax

H = 256
TILE = 128
TILES_DEV = 24
BOUND_DEV = 8
CAP = 3
KG = 4
KM = 8
EDGE_DEV = 2
HALO = 8
MEMBERS = 2
PARTITIONS = 4
MESH_TILES = 96
BOUND_TILES = 32


def draw_boundary_count(key, part):
    key = jax.random.fold_in(key, 11)
    first_key, second_key, third_key = jax.random.split(key, 3)
    counts = jax.random.randint(first_key, (PARTITIONS, PARTITIONS), 0, CAP + 1)
    row_pick = jax.random.randint(second_key, (), 0, PARTITIONS)
    column_pick = jax.random.randint(third_key, (), 0, PARTITIONS)
    return counts.at[row_pick, column_pick].set(CAP).astype(jnp.int32)


def draw_halo_count(key, part):
    key = jax.random.fold_in(key, 23)
    first_key, second_key = jax.random.split(key, 2)
    counts = jax.random.randint(first_key, (PARTITIONS,), 1, HALO + 1)
    row_pick = jax.random.randint(second_key, (), 0, PARTITIONS)
    return counts.at[row_pick].set(HALO).astype(jnp.int32)


def touch_ends(result, rng, least, largest):
    index_at = [jax.random.randint(jax.random.fold_in(rng, axis), (), 0, length) for axis, length in enumerate(result.shape)]
    longest = result.shape.index(max(result.shape))
    beside = index_at[:longest] + [(index_at[longest] + 1) % result.shape[longest]] + index_at[longest + 1:]
    return result.at[tuple(index_at)].set(least).at[tuple(beside)].set(largest)


def shard_levels(key, shape, cuts, least, high):
    factor_of, own = 1.0, jax.random.fold_in(key, 6)
    for position, blocks in cuts:
        steps = jnp.exp(jax.random.uniform(jax.random.fold_in(own, position), (blocks,), jnp.float32, least / len(cuts), high / len(cuts)))
        factor_of = factor_of * jnp.repeat(steps, shape[position] // blocks).reshape([-1 if axis == position else 1 for axis in range(len(shape))])
    return factor_of


def normal_values(key, dims, scale, bound, shards=(), kind=jnp.bfloat16):
    result = jax.random.normal(key, dims, jnp.float32) * scale
    if len(shards) > 0:
        result = shard_levels(key, dims, shards, -0.22, 0.18) * result
    return jnp.clip(result, min=-bound, max=bound).astype(kind)


def setup_inputs(seed: int = 0, part: int = 0) -> dict:
    key_list = jax.random.split(jax.random.key(seed), 17)
    part_splits = jax.random.split(jax.random.fold_in(key_list[16], part), 17)
    return {
        "mesh_state": normal_values(part_splits[0], (MEMBERS, MESH_TILES, TILE, H), 1.0, 6.0, ((0, 2), (1, 8))),
        "boundary": normal_values(part_splits[1], (MEMBERS, BOUND_TILES, TILE, H), 1.0, 6.0, ((0, 2), (1, 4))),
        "boundary_send": touch_ends(jax.random.randint(part_splits[2], (PARTITIONS, PARTITIONS, CAP), 0, BOUND_DEV), jax.random.fold_in(part_splits[2], 1), 0, BOUND_DEV - 1).astype(jnp.int32),
        "boundary_count": draw_boundary_count(jax.random.fold_in(jax.random.fold_in(key_list[16], part), 71), part),
        "grid_edges": touch_ends(jax.random.randint(part_splits[4], (MESH_TILES, KG), 0, PARTITIONS * CAP), jax.random.fold_in(part_splits[4], 1), 0, (PARTITIONS * CAP) - 1).astype(jnp.int32),
        "edge_tiles": touch_ends(jax.random.randint(part_splits[5], (PARTITIONS * EDGE_DEV,), 0, TILES_DEV), jax.random.fold_in(part_splits[5], 1), 0, TILES_DEV - 1).astype(jnp.int32),
        "halo_source": touch_ends(jax.random.randint(part_splits[6], (PARTITIONS * HALO,), 0, PARTITIONS * EDGE_DEV), jax.random.fold_in(part_splits[6], 1), 0, (PARTITIONS * EDGE_DEV) - 1).astype(jnp.int32),
        "halo_count": draw_halo_count(jax.random.fold_in(jax.random.fold_in(key_list[16], part), 71), part),
        "mesh_edges": touch_ends(jax.random.randint(part_splits[8], (MESH_TILES, KM), 0, TILES_DEV + HALO), jax.random.fold_in(part_splits[8], 1), 0, (TILES_DEV + HALO) - 1).astype(jnp.int32),
        "edge_first": normal_values(key_list[9], (2, 2, H, H), (2 * H) ** -0.5, 0.25),
        "edge_bias": normal_values(key_list[10], (2, H), 0.5, 3.0, (), jnp.float32),
        "edge_second": normal_values(key_list[11], (2, H, H), (H * KM) ** -0.5, 0.125),
        "node_first": normal_values(key_list[12], (2, 2, H, H), (2 * H) ** -0.5, 0.25),
        "node_bias": normal_values(key_list[13], (2, H), 0.5, 3.0, (), jnp.float32),
        "node_second": normal_values(key_list[14], (2, H, H), H ** -0.5, 0.375),
        "node_gain": jnp.clip(1.0 + 0.18 * jax.random.normal(key_list[15], (2, H), jnp.float32), 0.1, 1.9),
    }


def layer_norm(values, gain):
    center = values - lax.optimization_barrier(jnp.mean(values, axis=-1, keepdims=True))
    spread = lax.optimization_barrier(jnp.mean(center * center, axis=-1, keepdims=True))
    return center * lax.rsqrt(spread + 1e-05) * gain

def project(tiles, weight):
    return jnp.einsum('mtrh,hk->mtrk', tiles.astype(jnp.float32), weight.astype(jnp.float32))

def interact(targets, sources, edge_index, layer_id, edge_first, edge_bias, edge_second, node_first, node_bias, node_second, node_gain):
    source_proj = project(sources, edge_first[layer_id, 0])
    target_proj = project(targets, edge_first[layer_id, 1]) + edge_bias[layer_id]
    running = jnp.zeros(target_proj.shape, jnp.float32)
    for column in range(edge_index.shape[1]):
        running = running + jax.nn.silu(jnp.take(source_proj, edge_index[:, column], axis=1) + target_proj)
    hidden = running.astype(jnp.bfloat16)
    aggregate = project(hidden, edge_second[layer_id]).astype(jnp.bfloat16)
    inner_hidden = jax.nn.silu(project(targets, node_first[layer_id, 0]) + project(aggregate, node_first[layer_id, 1]) + node_bias[layer_id]).astype(jnp.bfloat16)
    node_sum = project(inner_hidden, node_second[layer_id])
    return (targets.astype(jnp.float32) + layer_norm(node_sum, node_gain[layer_id])).astype(jnp.bfloat16)

def reference(mesh_state, boundary, boundary_send, boundary_count, grid_edges, edge_tiles, halo_source, halo_count, mesh_edges, edge_first, edge_bias, edge_second, node_first, node_bias, node_second, node_gain):
    weights = (edge_first, edge_bias, edge_second, node_first, node_bias, node_second, node_gain)
    owners = jnp.arange(PARTITIONS, dtype=jnp.int32)

    def encode(part_index):
        tile_rows = boundary_send[:, part_index, :]
        live_slot = jnp.arange(CAP, dtype=jnp.int32)[None, :] < boundary_count[:, part_index][:, None]
        global_rows = (owners[:, None] * BOUND_DEV + tile_rows).reshape(-1)
        picked = jnp.take(boundary, global_rows, axis=1)
        slot_tiles = jnp.where(live_slot.reshape(-1)[None, :, None, None], picked, jnp.zeros((), jnp.bfloat16))
        targets = lax.dynamic_slice_in_dim(mesh_state, (part_index * TILES_DEV).astype(jnp.int32), TILES_DEV, 1)
        edge_index = lax.dynamic_slice_in_dim(grid_edges, (part_index * TILES_DEV).astype(jnp.int32), TILES_DEV, 0)
        return interact(targets, slot_tiles, edge_index, 0, *weights)
    encoded = lax.map(encode, owners)
    encoded = jnp.moveaxis(encoded, 0, 1).reshape(MEMBERS, MESH_TILES, TILE, H)
    edge_global = (jnp.repeat(owners, EDGE_DEV) * TILES_DEV + edge_tiles).astype(jnp.int32)
    edge_states = jnp.take(encoded, edge_global, axis=1)

    def process(part_index):
        wanted = lax.dynamic_slice_in_dim(halo_source, (part_index * HALO).astype(jnp.int32), HALO, 0)
        live_slot = jnp.arange(HALO, dtype=jnp.int32) < halo_count[part_index]
        halo_tiles = jnp.where(live_slot[None, :, None, None], jnp.take(edge_states, wanted, axis=1), jnp.zeros((), jnp.bfloat16))
        targets = lax.dynamic_slice_in_dim(encoded, (part_index * TILES_DEV).astype(jnp.int32), TILES_DEV, 1)
        sources = jnp.concatenate([targets, halo_tiles], axis=1)
        edge_index = lax.dynamic_slice_in_dim(mesh_edges, (part_index * TILES_DEV).astype(jnp.int32), TILES_DEV, 0)
        return interact(targets, sources, edge_index, 1, *weights)
    processed = lax.map(process, owners)
    return jnp.moveaxis(processed, 0, 1).reshape(MEMBERS, MESH_TILES, TILE, H)
```

```python
import functools

import jax
import jax.numpy as jnp
from jax import lax
from jax.experimental import pallas as pl
from jax.experimental.pallas import tpu as pltpu
from jax.sharding import PartitionSpec as P

MESH = pl.DeviceIdType.MESH
ROWS = 16
UNROLL = 4


def dot(left, right):
    return jnp.dot(left, right, preferred_element_type=jnp.float32)


def kernel(
    n,
    mesh_state,
    boundary,
    grid_edges,
    mesh_edges,
    boundary_send,
    boundary_count,
    edge_tiles,
    halo_source,
    halo_count,
    edge_first,
    edge_second,
    node_first,
    node_second,
    edge_bias,
    node_bias,
    node_gain,
    out,
    bound,
    picked,
    slots,
    targets,
    encoded,
    edge_out,
    edge_in,
    result,
    first,
    second,
    node_a,
    node_b,
    source_proj,
    target_proj,
    hidden,
    own_grid,
    own_mesh,
    far_grid,
    far_mesh,
    grid_index,
    mesh_index,
    halo_table,
    local_sem,
    state_sem,
    state_send,
    state_recv,
    index_send,
    index_recv,
    slot_send,
    slot_recv,
    halo_send,
    halo_recv,
    out_local,
    out_send,
    out_recv,
):
    space, chan = lax.axis_index("space"), lax.axis_index("chan")
    other = 1 - chan
    half = bound.shape[1]
    chunks = half // ROWS
    tiles_own = mesh_state.shape[1]
    tiles = 2 * tiles_own
    cap = boundary_send.shape[2]
    edges = edge_tiles.shape[0]
    halo = halo_source.shape[0]
    zero_tile = source_proj.shape[0] - 1
    features = targets.shape[2]

    def start_row(side, chunk):
        return pl.multiple_of(side * half + chunk * ROWS, ROWS)

    get_bound = pltpu.make_async_copy(
        boundary.at[0, :, pl.ds(start_row(chan, 0), half), :], bound, local_sem.at[0]
    )
    get_bound.start()
    index_copies = [
        pltpu.make_async_copy(grid_edges, own_grid, local_sem.at[1]),
        pltpu.make_async_copy(mesh_edges, own_mesh, local_sem.at[2]),
    ]
    weight_copies = [
        pltpu.make_async_copy(edge_first, first, local_sem.at[3]),
        pltpu.make_async_copy(edge_second, second, local_sem.at[4]),
        pltpu.make_async_copy(node_first, node_a, local_sem.at[5]),
        pltpu.make_async_copy(node_second, node_b, local_sem.at[6]),
    ]
    state_local = pltpu.make_async_copy(
        mesh_state.at[0, :, pl.ds(start_row(chan, 0), half), :],
        targets.at[pl.ds(chan * tiles_own, tiles_own)],
        state_sem,
    )
    state_local.start()
    for copy in index_copies + weight_copies:
        copy.start()

    barrier = pltpu.get_barrier_semaphore()
    for step in range(1, n):
        pl.semaphore_signal(
            barrier, inc=1, device_id={"space": lax.rem(space + step, n)}, device_id_type=MESH
        )
    pl.semaphore_signal(barrier, inc=1, device_id={"chan": other}, device_id_type=MESH)

    get_bound.wait()

    def pick(partition, chunk):
        values = []
        for c in range(cap):
            tile = bound[boundary_send[space, partition, c], pl.ds(chunk * ROWS, ROWS), :]
            live = jnp.where(c < boundary_count[space, partition], 1.0, 0.0)
            values.append((tile.astype(jnp.float32) * live).astype(jnp.bfloat16))
        return values

    for chunk in range(chunks):
        for step in range(1, n):
            for c, value in enumerate(pick(lax.rem(space + step, n), chunk)):
                picked[chunk, step - 1, c] = value

    pl.semaphore_wait(barrier, n)

    sends = []
    slot_copies = []
    for chunk in range(chunks):
        row = []
        for step in range(1, n):
            copy = pltpu.make_async_remote_copy(
                src_ref=picked.at[chunk, step - 1],
                dst_ref=slots.at[chunk, space],
                send_sem=slot_send.at[chunk, step - 1],
                recv_sem=slot_recv.at[chunk, step - 1],
                device_id={"space": lax.rem(space + step, n)},
                device_id_type=MESH,
            )
            copy.start()
            row.append(copy)
        slot_copies.append(row)
        sends += row

    far_index = []
    for number, (source, target) in enumerate(((grid_edges, far_grid), (mesh_edges, far_mesh))):
        copy = pltpu.make_async_remote_copy(
            src_ref=source,
            dst_ref=target,
            send_sem=index_send.at[number],
            recv_sem=index_recv.at[number],
            device_id={"chan": other},
            device_id_type=MESH,
        )
        copy.start()
        far_index.append(copy)
    sends += far_index
    state_copies = []
    for chunk in range(chunks):
        copy = pltpu.make_async_remote_copy(
            src_ref=mesh_state.at[0, :, pl.ds(start_row(other, chunk), ROWS), :],
            dst_ref=targets.at[pl.ds(chan * tiles_own, tiles_own), pl.ds(chunk * ROWS, ROWS), :],
            send_sem=state_send.at[chunk],
            recv_sem=state_recv.at[chunk],
            device_id={"chan": other},
            device_id_type=MESH,
        )
        copy.start()
        state_copies.append(copy)
    sends += state_copies

    for chunk in range(chunks):
        for c, value in enumerate(pick(space, chunk)):
            slots[chunk, space, c] = value
    for tile in range(tiles):
        halo_table[tile] = tile
    for h in range(halo):
        halo_table[tiles + h] = jnp.where(
            h < halo_count[0], tiles + halo_source[h], zero_tile
        )
    source_proj[zero_tile] = jnp.zeros((ROWS, features), jnp.float32)
    for copy in index_copies:
        copy.wait()
    for copy in far_index:
        copy.wait_recv()

    def index_step(tile, carry):
        near, far = chan * tiles_own + tile, other * tiles_own + tile
        for k in range(grid_index.shape[1]):
            grid_index[near, k] = own_grid[tile, k]
            grid_index[far, k] = far_grid[tile, k]
        for k in range(mesh_index.shape[1]):
            mesh_index[near, k] = halo_table[own_mesh[tile, k]]
            mesh_index[far, k] = halo_table[far_mesh[tile, k]]
        return carry

    lax.fori_loop(0, tiles_own, index_step, 0)
    for copy in weight_copies:
        copy.wait()
    state_local.wait()

    def interact(layer, target, index):
        target_proj[...] = (
            (dot(target, first[layer, 1]) + edge_bias[layer : layer + 1, :]) * 0.5
        ).reshape(target_proj.shape)

        def tile_step(tile, carry):
            base = target_proj[tile]
            total = None
            for k in range(index.shape[1]):
                value = source_proj[index[tile, k]] + base
                term = value * jnp.tanh(value) + value
                total = term if total is None else total + term
            hidden[tile] = total.astype(jnp.bfloat16)
            return carry

        lax.fori_loop(0, tiles, tile_step, 0, unroll=UNROLL)
        sums = hidden[...].reshape(tiles * ROWS, features)
        aggregate = dot(sums, second[layer]).astype(jnp.bfloat16)
        value = 0.5 * (
            dot(target, node_a[layer, 0])
            + dot(aggregate, node_a[layer, 1])
            + node_bias[layer : layer + 1, :]
        )
        inner = (value * jnp.tanh(value) + value).astype(jnp.bfloat16)
        node_sum = dot(inner, node_b[layer])
        center = node_sum - jnp.mean(node_sum, axis=-1, keepdims=True)
        spread = jnp.mean(center * center, axis=-1, keepdims=True)
        normed = center * lax.rsqrt(spread + 1e-05) * node_gain[layer : layer + 1, :]
        return (target.astype(jnp.float32) + normed).astype(jnp.bfloat16)

    def project(tiles_in, layer, begin):
        count = tiles_in.shape[0] // ROWS
        source_proj[begin : begin + count] = (dot(tiles_in, first[layer, 0]) * 0.5).reshape(
            count, ROWS, features
        )

    halo_copies = []

    def encode(chunk):
        rows = pl.ds(chunk * ROWS, ROWS)
        state_copies[chunk].wait_recv()
        for copy in slot_copies[chunk]:
            copy.wait_recv()
        project(slots[chunk].reshape(n * cap * ROWS, features), 0, 0)
        target = targets[:, rows, :].reshape(tiles * ROWS, features)
        encoded[:, rows, :] = interact(0, target, grid_index).reshape(tiles, ROWS, features)
        for j in range(edges):
            value = encoded[edge_tiles[j], rows, :]
            edge_out[chunk, j] = value
            edge_in[chunk, space, j] = value
        row = []
        for step in range(1, n):
            copy = pltpu.make_async_remote_copy(
                src_ref=edge_out.at[chunk],
                dst_ref=edge_in.at[chunk, space],
                send_sem=halo_send.at[chunk, step - 1],
                recv_sem=halo_recv.at[chunk, step - 1],
                device_id={"space": lax.rem(space + step, n)},
                device_id_type=MESH,
            )
            copy.start()
            row.append(copy)
        halo_copies.append(row)

    local_outs, far_outs = [], []

    def process(chunk):
        rows = pl.ds(chunk * ROWS, ROWS)
        target = encoded[:, rows, :].reshape(tiles * ROWS, features)
        project(target, 1, 0)
        for copy in halo_copies[chunk]:
            copy.wait_recv()
        project(edge_in[chunk].reshape(n * edges * ROWS, features), 1, tiles)
        result[:, rows, :] = interact(1, target, mesh_index).reshape(tiles, ROWS, features)
        place = out.at[0, :, pl.ds(start_row(chan, chunk), ROWS), :]
        far = pltpu.make_async_remote_copy(
            src_ref=result.at[pl.ds(other * tiles_own, tiles_own), rows, :],
            dst_ref=place,
            send_sem=out_send.at[chunk],
            recv_sem=out_recv.at[chunk],
            device_id={"chan": other},
            device_id_type=MESH,
        )
        far.start()
        far_outs.append(far)
        near = pltpu.make_async_copy(
            result.at[pl.ds(chan * tiles_own, tiles_own), rows, :], place, out_local.at[chunk]
        )
        near.start()
        local_outs.append(near)

    for chunk in range(chunks):
        encode(chunk)
    for chunk in range(chunks):
        process(chunk)

    for copy in sends:
        copy.wait_send()
    for row in halo_copies:
        for copy in row:
            copy.wait_send()
    for copy in local_outs + far_outs:
        copy.wait()


def body(
    n,
    mesh_state,
    boundary,
    boundary_send,
    boundary_count,
    grid_edges,
    edge_tiles,
    halo_source,
    halo_count,
    mesh_edges,
    edge_first,
    edge_bias,
    edge_second,
    node_first,
    node_bias,
    node_second,
    node_gain,
):
    _, own, tile, features = mesh_state.shape
    half = tile // 2
    chunks = half // ROWS
    tiles = 2 * own
    cap = boundary_send.shape[2]
    edges = edge_tiles.shape[0]
    halo = halo_source.shape[0]
    count = max(n * cap, tiles + n * edges) + 1
    bf16, f32, i32 = jnp.bfloat16, jnp.float32, jnp.int32
    dma = pltpu.SemaphoreType.DMA
    scratch = [
        pltpu.VMEM((boundary.shape[1], half, features), bf16),
        pltpu.VMEM((chunks, n - 1, cap, ROWS, features), bf16),
        pltpu.VMEM((chunks, n, cap, ROWS, features), bf16),
        pltpu.VMEM((tiles, half, features), bf16),
        pltpu.VMEM((tiles, half, features), bf16),
        pltpu.VMEM((chunks, edges, ROWS, features), bf16),
        pltpu.VMEM((chunks, n, edges, ROWS, features), bf16),
        pltpu.VMEM((tiles, half, features), bf16),
        pltpu.VMEM(edge_first.shape, bf16),
        pltpu.VMEM(edge_second.shape, bf16),
        pltpu.VMEM(node_first.shape, bf16),
        pltpu.VMEM(node_second.shape, bf16),
        pltpu.VMEM((count, ROWS, features), f32),
        pltpu.VMEM((tiles, ROWS, features), f32),
        pltpu.VMEM((tiles, ROWS, features), bf16),
        pltpu.SMEM(grid_edges.shape, i32),
        pltpu.SMEM(mesh_edges.shape, i32),
        pltpu.SMEM(grid_edges.shape, i32),
        pltpu.SMEM(mesh_edges.shape, i32),
        pltpu.SMEM((tiles, grid_edges.shape[1]), i32),
        pltpu.SMEM((tiles, mesh_edges.shape[1]), i32),
        pltpu.SMEM((tiles + halo,), i32),
        dma((7,)),
        dma,
        dma((chunks,)),
        dma((chunks,)),
        dma((2,)),
        dma((2,)),
        dma((chunks, n - 1)),
        dma((chunks, n - 1)),
        dma((chunks, n - 1)),
        dma((chunks, n - 1)),
        dma((chunks,)),
        dma((chunks,)),
        dma((chunks,)),
    ]
    hbm = pl.BlockSpec(memory_space=pl.ANY)
    smem = pl.BlockSpec(memory_space=pltpu.SMEM)
    vmem = pl.BlockSpec(memory_space=pltpu.VMEM)
    return pl.pallas_call(
        functools.partial(kernel, n),
        out_shape=jax.ShapeDtypeStruct(mesh_state.shape, bf16),
        in_specs=[hbm] * 4 + [smem] * 5 + [hbm] * 4 + [vmem] * 3,
        out_specs=hbm,
        scratch_shapes=scratch,
        compiler_params=pltpu.CompilerParams(
            collective_id=0, has_side_effects=True, vmem_limit_bytes=40 * 1024 * 1024
        ),
    )(
        mesh_state,
        boundary,
        grid_edges,
        mesh_edges,
        boundary_send,
        boundary_count,
        edge_tiles,
        halo_source,
        halo_count,
        edge_first,
        edge_second,
        node_first,
        node_second,
        edge_bias,
        node_bias,
        node_gain,
    )


def solution(mesh):
    in_specs = (
        P(("groups", "member"), ("space", "chan"), None, None),
        P(("groups", "member"), "space", None, None),
        P("groups", None, None),
        P("groups", None),
        P(("groups", "space", "chan"), None),
        P(("groups", "space")),
        P(("groups", "space")),
        P(("groups", "space")),
        P(("groups", "space", "chan"), None),
        P(),
        P(),
        P(),
        P(),
        P(),
        P(),
        P(),
    )
    out_specs = P(("groups", "member"), ("space", "chan"), None, None)
    return jax.shard_map(
        functools.partial(body, mesh.shape["space"]),
        mesh=mesh,
        in_specs=in_specs,
        out_specs=out_specs,
        check_vma=False,
    )
```

```python
import functools

import jax
import jax.numpy as jnp
from jax import lax
from jax.experimental import pallas as pl
from jax.experimental.pallas import tpu as pltpu
from jax.sharding import PartitionSpec as P

MESH = pl.DeviceIdType.MESH
ROWS = 32
UNROLL = 4
SEND_ORDER = (2, 0, 1)


def dot(left, right):
    return jnp.dot(left, right, preferred_element_type=jnp.float32)


def kernel(
    n,
    mesh_state,
    boundary,
    grid_edges,
    mesh_edges,
    boundary_send_in,
    boundary_count_in,
    edge_tiles_in,
    halo_source_in,
    halo_count_in,
    edge_first,
    edge_second,
    node_first,
    node_second,
    edge_bias_in,
    node_bias_in,
    node_gain_in,
    out,
    boundary_send,
    boundary_count,
    edge_tiles,
    halo_source,
    halo_count,
    edge_bias,
    node_bias,
    node_gain,
    bound,
    picked,
    slots,
    targets,
    encoded,
    edge_out,
    edge_in,
    result,
    first,
    second,
    node_a,
    node_b,
    source_proj,
    target_proj,
    hidden,
    own_grid,
    own_mesh,
    far_grid,
    far_mesh,
    grid_index,
    mesh_index,
    halo_table,
    local_sem,
    state_sem,
    state_send,
    state_recv,
    index_send,
    index_recv,
    slot_send,
    slot_recv,
    halo_send,
    halo_recv,
    out_local,
    out_send,
    out_recv,
):
    space, chan = lax.axis_index("space"), lax.axis_index("chan")
    other = 1 - chan
    half = bound.shape[1]
    chunks = half // ROWS
    tiles_own = mesh_state.shape[1]
    tiles = 2 * tiles_own
    cap = boundary_send.shape[0]
    edges = edge_tiles.shape[0]
    halo = halo_source.shape[0]
    zero_tile = source_proj.shape[0] - 1
    features = targets.shape[2]

    def start_row(side, chunk):
        return pl.multiple_of(side * half + chunk * ROWS, ROWS)

    get_bound = pltpu.make_async_copy(
        boundary.at[0, :, pl.ds(start_row(chan, 0), half), :], bound, local_sem.at[0]
    )
    get_bound.start()
    table_copies = [
        pltpu.make_async_copy(boundary_send_in, boundary_send, local_sem.at[7]),
        pltpu.make_async_copy(boundary_count_in, boundary_count, local_sem.at[8]),
    ]
    for copy in table_copies:
        copy.start()
    index_copies = [
        pltpu.make_async_copy(edge_tiles_in, edge_tiles, local_sem.at[9]),
        pltpu.make_async_copy(halo_source_in, halo_source, local_sem.at[10]),
        pltpu.make_async_copy(halo_count_in, halo_count, local_sem.at[11]),
        pltpu.make_async_copy(grid_edges, own_grid, local_sem.at[1]),
        pltpu.make_async_copy(mesh_edges, own_mesh, local_sem.at[2]),
    ]
    weight_copies = [
        pltpu.make_async_copy(edge_bias_in, edge_bias, local_sem.at[12]),
        pltpu.make_async_copy(node_bias_in, node_bias, local_sem.at[13]),
        pltpu.make_async_copy(node_gain_in, node_gain, local_sem.at[14]),
        pltpu.make_async_copy(edge_first, first, local_sem.at[3]),
        pltpu.make_async_copy(edge_second, second, local_sem.at[4]),
        pltpu.make_async_copy(node_first, node_a, local_sem.at[5]),
        pltpu.make_async_copy(node_second, node_b, local_sem.at[6]),
    ]
    state_local = pltpu.make_async_copy(
        mesh_state.at[0, :, pl.ds(start_row(chan, 0), half), :],
        targets.at[pl.ds(chan * tiles_own, tiles_own)],
        state_sem,
    )
    state_local.start()
    for copy in index_copies + weight_copies:
        copy.start()

    barrier = pltpu.get_barrier_semaphore()
    for step in range(1, n):
        pl.semaphore_signal(
            barrier, inc=1, device_id={"space": lax.rem(space + step, n)}, device_id_type=MESH
        )
    pl.semaphore_signal(barrier, inc=1, device_id={"chan": other}, device_id_type=MESH)

    get_bound.wait()
    for copy in table_copies:
        copy.wait()

    def pick(partition, chunk):
        values = []
        for c in range(cap):
            tile = bound[boundary_send[c, space, partition], pl.ds(chunk * ROWS, ROWS), :]
            live = jnp.where(c < boundary_count[space, partition], 1.0, 0.0)
            values.append((tile.astype(jnp.float32) * live).astype(jnp.bfloat16))
        return values

    for chunk in range(chunks):
        for step in range(1, n):
            for c, value in enumerate(pick(lax.rem(space + step, n), chunk)):
                picked[chunk, step - 1, c] = value

    pl.semaphore_wait(barrier, n)

    sends = []
    slot_copies = []
    for chunk in range(chunks):
        row = []
        for step in range(1, n):
            copy = pltpu.make_async_remote_copy(
                src_ref=picked.at[chunk, step - 1],
                dst_ref=slots.at[chunk, space],
                send_sem=slot_send.at[chunk, step - 1],
                recv_sem=slot_recv.at[chunk, step - 1],
                device_id={"space": lax.rem(space + step, n)},
                device_id_type=MESH,
            )
            copy.start()
            row.append(copy)
        slot_copies.append(row)
        sends += row

    far_index = []
    for number, (source, target) in enumerate(((grid_edges, far_grid), (mesh_edges, far_mesh))):
        copy = pltpu.make_async_remote_copy(
            src_ref=source,
            dst_ref=target,
            send_sem=index_send.at[number],
            recv_sem=index_recv.at[number],
            device_id={"chan": other},
            device_id_type=MESH,
        )
        copy.start()
        far_index.append(copy)
    sends += far_index
    state_copies = []
    for chunk in range(chunks):
        copy = pltpu.make_async_remote_copy(
            src_ref=mesh_state.at[0, :, pl.ds(start_row(other, chunk), ROWS), :],
            dst_ref=targets.at[pl.ds(chan * tiles_own, tiles_own), pl.ds(chunk * ROWS, ROWS), :],
            send_sem=state_send.at[chunk],
            recv_sem=state_recv.at[chunk],
            device_id={"chan": other},
            device_id_type=MESH,
        )
        copy.start()
        state_copies.append(copy)
    sends += state_copies

    for chunk in range(chunks):
        for c, value in enumerate(pick(space, chunk)):
            slots[chunk, space, c] = value
    for copy in index_copies:
        copy.wait()
    for tile in range(tiles):
        halo_table[tile] = tile
    for h in range(halo):
        halo_table[tiles + h] = jnp.where(
            h < halo_count[0], tiles + halo_source[h], zero_tile
        )
    source_proj[zero_tile] = jnp.zeros((ROWS, features), jnp.float32)
    for copy in far_index:
        copy.wait_recv()

    def index_step(tile, carry):
        near, far = chan * tiles_own + tile, other * tiles_own + tile
        for k in range(grid_index.shape[1]):
            grid_index[near, k] = own_grid[k, tile]
            grid_index[far, k] = far_grid[k, tile]
        for k in range(mesh_index.shape[1]):
            mesh_index[near, k] = halo_table[own_mesh[k, tile]]
            mesh_index[far, k] = halo_table[far_mesh[k, tile]]
        return carry

    lax.fori_loop(0, tiles_own, index_step, 0)
    for copy in weight_copies:
        copy.wait()
    state_local.wait()

    def interact(layer, target, index):
        target_proj[...] = (
            (dot(target, first[layer, 1]) + edge_bias[layer : layer + 1, :]) * 0.5
        ).reshape(target_proj.shape)

        def tile_step(tile, carry):
            base = target_proj[tile]
            total = None
            for k in range(index.shape[1]):
                value = source_proj[index[tile, k]] + base
                term = value * jnp.tanh(value) + value
                total = term if total is None else total + term
            hidden[tile] = total.astype(jnp.bfloat16)
            return carry

        lax.fori_loop(0, tiles, tile_step, 0, unroll=UNROLL)
        sums = hidden[...].reshape(tiles * ROWS, features)
        aggregate = dot(sums, second[layer]).astype(jnp.bfloat16)
        value = 0.5 * (
            dot(target, node_a[layer, 0])
            + dot(aggregate, node_a[layer, 1])
            + node_bias[layer : layer + 1, :]
        )
        inner = (value * jnp.tanh(value) + value).astype(jnp.bfloat16)
        node_sum = dot(inner, node_b[layer])
        center = node_sum - jnp.mean(node_sum, axis=-1, keepdims=True)
        spread = jnp.mean(center * center, axis=-1, keepdims=True)
        normed = center * lax.rsqrt(spread + 1e-05) * node_gain[layer : layer + 1, :]
        return (target.astype(jnp.float32) + normed).astype(jnp.bfloat16)

    def project(tiles_in, layer, begin):
        count = tiles_in.shape[0] // ROWS
        source_proj[begin : begin + count] = (dot(tiles_in, first[layer, 0]) * 0.5).reshape(
            count, ROWS, features
        )

    halo_copies = []

    def encode(chunk):
        rows = pl.ds(chunk * ROWS, ROWS)
        state_copies[chunk].wait_recv()
        for copy in slot_copies[chunk]:
            copy.wait_recv()
        project(slots[chunk].reshape(n * cap * ROWS, features), 0, 0)
        target = targets[:, rows, :].reshape(tiles * ROWS, features)
        encoded[:, rows, :] = interact(0, target, grid_index).reshape(tiles, ROWS, features)
        for j in range(edges):
            value = encoded[edge_tiles[j], rows, :]
            edge_out[chunk, j] = value
            edge_in[chunk, space, j] = value
        row = []
        for step in range(1, n):
            copy = pltpu.make_async_remote_copy(
                src_ref=edge_out.at[chunk],
                dst_ref=edge_in.at[chunk, space],
                send_sem=halo_send.at[chunk, step - 1],
                recv_sem=halo_recv.at[chunk, step - 1],
                device_id={"space": lax.rem(space + step, n)},
                device_id_type=MESH,
            )
            copy.start()
            row.append(copy)
        halo_copies.append(row)

    local_outs, far_outs = [], []

    def process(chunk):
        rows = pl.ds(chunk * ROWS, ROWS)
        target = encoded[:, rows, :].reshape(tiles * ROWS, features)
        project(target, 1, 0)
        for copy in halo_copies[chunk]:
            copy.wait_recv()
        project(edge_in[chunk].reshape(n * edges * ROWS, features), 1, tiles)
        result[:, rows, :] = interact(1, target, mesh_index).reshape(tiles, ROWS, features)
        place = out.at[0, :, pl.ds(start_row(chan, chunk), ROWS), :]
        far = pltpu.make_async_remote_copy(
            src_ref=result.at[pl.ds(other * tiles_own, tiles_own), rows, :],
            dst_ref=place,
            send_sem=out_send.at[chunk],
            recv_sem=out_recv.at[chunk],
            device_id={"chan": other},
            device_id_type=MESH,
        )
        far.start()
        far_outs.append(far)
        near = pltpu.make_async_copy(
            result.at[pl.ds(chan * tiles_own, tiles_own), rows, :], place, out_local.at[chunk]
        )
        near.start()
        local_outs.append(near)

    for chunk in range(chunks):
        encode(chunk)
    for chunk in range(chunks):
        process(chunk)

    for copy in sends:
        copy.wait_send()
    for row in halo_copies:
        for copy in row:
            copy.wait_send()
    for copy in local_outs + far_outs:
        copy.wait()


def body(
    n,
    mesh_state,
    boundary,
    boundary_send,
    boundary_count,
    grid_edges,
    edge_tiles,
    halo_source,
    halo_count,
    mesh_edges,
    edge_first,
    edge_bias,
    edge_second,
    node_first,
    node_bias,
    node_second,
    node_gain,
):
    _, own, tile, features = mesh_state.shape
    half = tile // 2
    chunks = half // ROWS
    tiles = 2 * own
    cap = boundary_send.shape[2]
    edges = edge_tiles.shape[0]
    halo = halo_source.shape[0]
    count = max(n * cap, tiles + n * edges) + 1
    bf16, f32, i32 = jnp.bfloat16, jnp.float32, jnp.int32
    dma = pltpu.SemaphoreType.DMA
    scratch = [
        pltpu.SMEM(tuple(boundary_send.shape[axis] for axis in SEND_ORDER), i32),
        pltpu.SMEM(boundary_count.shape, i32),
        pltpu.SMEM(edge_tiles.shape, i32),
        pltpu.SMEM(halo_source.shape, i32),
        pltpu.SMEM(halo_count.shape, i32),
        pltpu.VMEM(edge_bias.shape, f32),
        pltpu.VMEM(node_bias.shape, f32),
        pltpu.VMEM(node_gain.shape, f32),
        pltpu.VMEM((boundary.shape[1], half, features), bf16),
        pltpu.VMEM((chunks, n - 1, cap, ROWS, features), bf16),
        pltpu.VMEM((chunks, n, cap, ROWS, features), bf16),
        pltpu.VMEM((tiles, half, features), bf16),
        pltpu.VMEM((tiles, half, features), bf16),
        pltpu.VMEM((chunks, edges, ROWS, features), bf16),
        pltpu.VMEM((chunks, n, edges, ROWS, features), bf16),
        pltpu.VMEM((tiles, half, features), bf16),
        pltpu.VMEM(edge_first.shape, bf16),
        pltpu.VMEM(edge_second.shape, bf16),
        pltpu.VMEM(node_first.shape, bf16),
        pltpu.VMEM(node_second.shape, bf16),
        pltpu.VMEM((count, ROWS, features), f32),
        pltpu.VMEM((tiles, ROWS, features), f32),
        pltpu.VMEM((tiles, ROWS, features), bf16),
        pltpu.SMEM(grid_edges.shape[::-1], i32),
        pltpu.SMEM(mesh_edges.shape[::-1], i32),
        pltpu.SMEM(grid_edges.shape[::-1], i32),
        pltpu.SMEM(mesh_edges.shape[::-1], i32),
        pltpu.SMEM((tiles, grid_edges.shape[1]), i32),
        pltpu.SMEM((tiles, mesh_edges.shape[1]), i32),
        pltpu.SMEM((tiles + halo,), i32),
        dma((15,)),
        dma,
        dma((chunks,)),
        dma((chunks,)),
        dma((2,)),
        dma((2,)),
        dma((chunks, n - 1)),
        dma((chunks, n - 1)),
        dma((chunks, n - 1)),
        dma((chunks, n - 1)),
        dma((chunks,)),
        dma((chunks,)),
        dma((chunks,)),
    ]
    hbm = pl.BlockSpec(memory_space=pltpu.HBM)
    return pl.pallas_call(
        functools.partial(kernel, n),
        out_shape=jax.ShapeDtypeStruct(mesh_state.shape, bf16),
        in_specs=[hbm] * 16,
        out_specs=hbm,
        scratch_shapes=scratch,
        compiler_params=pltpu.CompilerParams(
            collective_id=0, has_side_effects=True, vmem_limit_bytes=60 * 1024 * 1024
        ),
    )(
        mesh_state,
        boundary,
        grid_edges.T,
        mesh_edges.T,
        jnp.transpose(boundary_send, SEND_ORDER),
        boundary_count,
        edge_tiles,
        halo_source,
        halo_count,
        edge_first,
        edge_second,
        node_first,
        node_second,
        edge_bias,
        node_bias,
        node_gain,
    )


def solution(mesh):
    in_specs = (
        P(("groups", "member"), ("space", "chan"), None, None),
        P(("groups", "member"), "space", None, None),
        P("groups", None, None),
        P("groups", None),
        P(("groups", "space", "chan"), None),
        P(("groups", "space")),
        P(("groups", "space")),
        P(("groups", "space")),
        P(("groups", "space", "chan"), None),
        P(),
        P(),
        P(),
        P(),
        P(),
        P(),
        P(),
    )
    out_specs = P(("groups", "member"), ("space", "chan"), None, None)
    return jax.shard_map(
        functools.partial(body, mesh.shape["space"]),
        mesh=mesh,
        in_specs=in_specs,
        out_specs=out_specs,
        check_vma=False,
    )
```

```python
import functools

import jax
import jax.numpy as jnp
from jax import lax
from jax.experimental import pallas as pl
from jax.experimental.pallas import tpu as pltpu
from jax.sharding import PartitionSpec as P

MESH = pl.DeviceIdType.MESH
ROWS = 32
UNROLL = 4
SEND_ORDER = (2, 0, 1)


def dot(left, right):
    return jnp.dot(left, right, preferred_element_type=jnp.float32)


def kernel(
    n,
    mesh_state,
    boundary,
    grid_edges,
    mesh_edges,
    boundary_send_in,
    boundary_count_in,
    edge_tiles_in,
    halo_source_in,
    halo_count_in,
    edge_first,
    edge_second,
    node_first,
    node_second,
    edge_bias_in,
    node_bias_in,
    node_gain_in,
    out,
    boundary_send,
    boundary_count,
    edge_tiles,
    halo_source,
    halo_count,
    edge_bias,
    node_bias,
    node_gain,
    bound,
    picked,
    slots,
    targets,
    encoded,
    edge_out,
    edge_in,
    result,
    first,
    second,
    node_a,
    node_b,
    source_proj,
    target_proj,
    hidden,
    own_grid,
    own_mesh,
    far_grid,
    far_mesh,
    grid_index,
    mesh_index,
    halo_table,
    local_sem,
    state_sem,
    state_send,
    state_recv,
    index_send,
    index_recv,
    slot_send,
    slot_recv,
    halo_send,
    halo_recv,
    out_local,
    out_send,
    out_recv,
):
    space, chan = lax.axis_index("space"), lax.axis_index("chan")
    other = 1 - chan
    half = bound.shape[1]
    chunks = half // ROWS
    tiles_own = mesh_state.shape[1]
    tiles = 2 * tiles_own
    cap = boundary_send.shape[0]
    edges = edge_tiles.shape[0]
    halo = halo_source.shape[0]
    zero_tile = source_proj.shape[0] - 1
    features = targets.shape[2]

    def start_row(side, chunk):
        return pl.multiple_of(side * half + chunk * ROWS, ROWS)

    barrier = pltpu.get_barrier_semaphore()
    for step in range(1, n):
        pl.semaphore_signal(
            barrier, inc=1, device_id={"space": lax.rem(space + step, n)}, device_id_type=MESH
        )
    pl.semaphore_signal(barrier, inc=1, device_id={"chan": other}, device_id_type=MESH)

    get_bound = pltpu.make_async_copy(
        boundary.at[0, :, pl.ds(start_row(chan, 0), half), :], bound, local_sem.at[0]
    )
    get_bound.start()
    table_copies = [
        pltpu.make_async_copy(boundary_send_in, boundary_send, local_sem.at[7]),
        pltpu.make_async_copy(boundary_count_in, boundary_count, local_sem.at[8]),
    ]
    for copy in table_copies:
        copy.start()
    index_copies = [
        pltpu.make_async_copy(edge_tiles_in, edge_tiles, local_sem.at[9]),
        pltpu.make_async_copy(halo_source_in, halo_source, local_sem.at[10]),
        pltpu.make_async_copy(halo_count_in, halo_count, local_sem.at[11]),
        pltpu.make_async_copy(grid_edges, own_grid, local_sem.at[1]),
        pltpu.make_async_copy(mesh_edges, own_mesh, local_sem.at[2]),
    ]
    weight_copies = [
        pltpu.make_async_copy(edge_bias_in, edge_bias, local_sem.at[12]),
        pltpu.make_async_copy(node_bias_in, node_bias, local_sem.at[13]),
        pltpu.make_async_copy(node_gain_in, node_gain, local_sem.at[14]),
        pltpu.make_async_copy(edge_first, first, local_sem.at[3]),
        pltpu.make_async_copy(edge_second, second, local_sem.at[4]),
        pltpu.make_async_copy(node_first, node_a, local_sem.at[5]),
        pltpu.make_async_copy(node_second, node_b, local_sem.at[6]),
    ]
    state_local = pltpu.make_async_copy(
        mesh_state.at[0, :, pl.ds(start_row(chan, 0), half), :],
        targets.at[pl.ds(chan * tiles_own, tiles_own)],
        state_sem,
    )
    state_local.start()
    for copy in index_copies + weight_copies:
        copy.start()

    get_bound.wait()
    for copy in table_copies:
        copy.wait()

    def pick(partition, chunk):
        values = []
        for c in range(cap):
            tile = bound[boundary_send[c, space, partition], pl.ds(chunk * ROWS, ROWS), :]
            live = jnp.where(c < boundary_count[space, partition], 1.0, 0.0)
            values.append((tile.astype(jnp.float32) * live).astype(jnp.bfloat16))
        return values

    sends = []
    slot_copies = []
    for chunk in range(chunks):
        for step in range(1, n):
            for c, value in enumerate(pick(lax.rem(space + step, n), chunk)):
                picked[chunk, step - 1, c] = value
        if chunk == 0:
            pl.semaphore_wait(barrier, n)
        row = []
        for step in range(1, n):
            copy = pltpu.make_async_remote_copy(
                src_ref=picked.at[chunk, step - 1],
                dst_ref=slots.at[chunk, space],
                send_sem=slot_send.at[chunk, step - 1],
                recv_sem=slot_recv.at[chunk, step - 1],
                device_id={"space": lax.rem(space + step, n)},
                device_id_type=MESH,
            )
            copy.start()
            row.append(copy)
        slot_copies.append(row)
        sends += row

    far_index = []
    for number, (source, target) in enumerate(((grid_edges, far_grid), (mesh_edges, far_mesh))):
        copy = pltpu.make_async_remote_copy(
            src_ref=source,
            dst_ref=target,
            send_sem=index_send.at[number],
            recv_sem=index_recv.at[number],
            device_id={"chan": other},
            device_id_type=MESH,
        )
        copy.start()
        far_index.append(copy)
    sends += far_index
    state_copies = []
    for chunk in range(chunks):
        copy = pltpu.make_async_remote_copy(
            src_ref=mesh_state.at[0, :, pl.ds(start_row(other, chunk), ROWS), :],
            dst_ref=targets.at[pl.ds(chan * tiles_own, tiles_own), pl.ds(chunk * ROWS, ROWS), :],
            send_sem=state_send.at[chunk],
            recv_sem=state_recv.at[chunk],
            device_id={"chan": other},
            device_id_type=MESH,
        )
        copy.start()
        state_copies.append(copy)
    sends += state_copies

    for chunk in range(chunks):
        for c, value in enumerate(pick(space, chunk)):
            slots[chunk, space, c] = value
    for copy in index_copies:
        copy.wait()
    for tile in range(tiles):
        halo_table[tile] = tile
    for h in range(halo):
        halo_table[tiles + h] = jnp.where(
            h < halo_count[0], tiles + halo_source[h], zero_tile
        )
    source_proj[zero_tile] = jnp.zeros((ROWS, features), jnp.float32)
    for copy in far_index:
        copy.wait_recv()

    def index_step(tile, carry):
        near, far = chan * tiles_own + tile, other * tiles_own + tile
        for k in range(grid_index.shape[1]):
            grid_index[near, k] = own_grid[k, tile]
            grid_index[far, k] = far_grid[k, tile]
        for k in range(mesh_index.shape[1]):
            mesh_index[near, k] = halo_table[own_mesh[k, tile]]
            mesh_index[far, k] = halo_table[far_mesh[k, tile]]
        return carry

    lax.fori_loop(0, tiles_own, index_step, 0)
    for copy in weight_copies:
        copy.wait()
    state_local.wait()

    def interact(layer, target, index):
        target_proj[...] = (
            (dot(target, first[layer, 1]) + edge_bias[layer : layer + 1, :]) * 0.5
        ).reshape(target_proj.shape)

        def tile_step(tile, carry):
            base = target_proj[tile]
            total = None
            for k in range(index.shape[1]):
                value = source_proj[index[tile, k]] + base
                term = value * jnp.tanh(value) + value
                total = term if total is None else total + term
            hidden[tile] = total.astype(jnp.bfloat16)
            return carry

        lax.fori_loop(0, tiles, tile_step, 0, unroll=UNROLL)
        sums = hidden[...].reshape(tiles * ROWS, features)
        aggregate = dot(sums, second[layer]).astype(jnp.bfloat16)
        value = 0.5 * (
            dot(target, node_a[layer, 0])
            + dot(aggregate, node_a[layer, 1])
            + node_bias[layer : layer + 1, :]
        )
        inner = (value * jnp.tanh(value) + value).astype(jnp.bfloat16)
        node_sum = dot(inner, node_b[layer])
        center = node_sum - jnp.mean(node_sum, axis=-1, keepdims=True)
        spread = jnp.mean(center * center, axis=-1, keepdims=True)
        normed = center * lax.rsqrt(spread + 1e-05) * node_gain[layer : layer + 1, :]
        return (target.astype(jnp.float32) + normed).astype(jnp.bfloat16)

    def project(tiles_in, layer, begin):
        count = tiles_in.shape[0] // ROWS
        source_proj[begin : begin + count] = (dot(tiles_in, first[layer, 0]) * 0.5).reshape(
            count, ROWS, features
        )

    halo_copies = []

    def encode(chunk):
        rows = pl.ds(chunk * ROWS, ROWS)
        state_copies[chunk].wait_recv()
        for copy in slot_copies[chunk]:
            copy.wait_recv()
        project(slots[chunk].reshape(n * cap * ROWS, features), 0, 0)
        target = targets[:, rows, :].reshape(tiles * ROWS, features)
        encoded[:, rows, :] = interact(0, target, grid_index).reshape(tiles, ROWS, features)
        for j in range(edges):
            value = encoded[edge_tiles[j], rows, :]
            edge_out[chunk, j] = value
            edge_in[chunk, space, j] = value
        row = []
        for step in range(1, n):
            copy = pltpu.make_async_remote_copy(
                src_ref=edge_out.at[chunk],
                dst_ref=edge_in.at[chunk, space],
                send_sem=halo_send.at[chunk, step - 1],
                recv_sem=halo_recv.at[chunk, step - 1],
                device_id={"space": lax.rem(space + step, n)},
                device_id_type=MESH,
            )
            copy.start()
            row.append(copy)
        halo_copies.append(row)

    local_outs, far_outs = [], []

    def process(chunk):
        rows = pl.ds(chunk * ROWS, ROWS)
        target = encoded[:, rows, :].reshape(tiles * ROWS, features)
        project(target, 1, 0)
        for copy in halo_copies[chunk]:
            copy.wait_recv()
        project(edge_in[chunk].reshape(n * edges * ROWS, features), 1, tiles)
        result[:, rows, :] = interact(1, target, mesh_index).reshape(tiles, ROWS, features)
        place = out.at[0, :, pl.ds(start_row(chan, chunk), ROWS), :]
        far = pltpu.make_async_remote_copy(
            src_ref=result.at[pl.ds(other * tiles_own, tiles_own), rows, :],
            dst_ref=place,
            send_sem=out_send.at[chunk],
            recv_sem=out_recv.at[chunk],
            device_id={"chan": other},
            device_id_type=MESH,
        )
        far.start()
        far_outs.append(far)
        near = pltpu.make_async_copy(
            result.at[pl.ds(chan * tiles_own, tiles_own), rows, :], place, out_local.at[chunk]
        )
        near.start()
        local_outs.append(near)

    for chunk in range(chunks):
        encode(chunk)
    for chunk in range(chunks):
        process(chunk)

    for copy in sends:
        copy.wait_send()
    for row in halo_copies:
        for copy in row:
            copy.wait_send()
    for copy in local_outs + far_outs:
        copy.wait()


def body(
    n,
    mesh_state,
    boundary,
    boundary_send,
    boundary_count,
    grid_edges,
    edge_tiles,
    halo_source,
    halo_count,
    mesh_edges,
    edge_first,
    edge_bias,
    edge_second,
    node_first,
    node_bias,
    node_second,
    node_gain,
):
    _, own, tile, features = mesh_state.shape
    half = tile // 2
    chunks = half // ROWS
    tiles = 2 * own
    cap = boundary_send.shape[2]
    edges = edge_tiles.shape[0]
    halo = halo_source.shape[0]
    count = max(n * cap, tiles + n * edges) + 1
    bf16, f32, i32 = jnp.bfloat16, jnp.float32, jnp.int32
    dma = pltpu.SemaphoreType.DMA
    scratch = [
        pltpu.SMEM(tuple(boundary_send.shape[axis] for axis in SEND_ORDER), i32),
        pltpu.SMEM(boundary_count.shape, i32),
        pltpu.SMEM(edge_tiles.shape, i32),
        pltpu.SMEM(halo_source.shape, i32),
        pltpu.SMEM(halo_count.shape, i32),
        pltpu.VMEM(edge_bias.shape, f32),
        pltpu.VMEM(node_bias.shape, f32),
        pltpu.VMEM(node_gain.shape, f32),
        pltpu.VMEM((boundary.shape[1], half, features), bf16),
        pltpu.VMEM((chunks, n - 1, cap, ROWS, features), bf16),
        pltpu.VMEM((chunks, n, cap, ROWS, features), bf16),
        pltpu.VMEM((tiles, half, features), bf16),
        pltpu.VMEM((tiles, half, features), bf16),
        pltpu.VMEM((chunks, edges, ROWS, features), bf16),
        pltpu.VMEM((chunks, n, edges, ROWS, features), bf16),
        pltpu.VMEM((tiles, half, features), bf16),
        pltpu.VMEM(edge_first.shape, bf16),
        pltpu.VMEM(edge_second.shape, bf16),
        pltpu.VMEM(node_first.shape, bf16),
        pltpu.VMEM(node_second.shape, bf16),
        pltpu.VMEM((count, ROWS, features), f32),
        pltpu.VMEM((tiles, ROWS, features), f32),
        pltpu.VMEM((tiles, ROWS, features), bf16),
        pltpu.SMEM(grid_edges.shape[::-1], i32),
        pltpu.SMEM(mesh_edges.shape[::-1], i32),
        pltpu.SMEM(grid_edges.shape[::-1], i32),
        pltpu.SMEM(mesh_edges.shape[::-1], i32),
        pltpu.SMEM((tiles, grid_edges.shape[1]), i32),
        pltpu.SMEM((tiles, mesh_edges.shape[1]), i32),
        pltpu.SMEM((tiles + halo,), i32),
        dma((15,)),
        dma,
        dma((chunks,)),
        dma((chunks,)),
        dma((2,)),
        dma((2,)),
        dma((chunks, n - 1)),
        dma((chunks, n - 1)),
        dma((chunks, n - 1)),
        dma((chunks, n - 1)),
        dma((chunks,)),
        dma((chunks,)),
        dma((chunks,)),
    ]
    hbm = pl.BlockSpec(memory_space=pltpu.HBM)
    return pl.pallas_call(
        functools.partial(kernel, n),
        out_shape=pltpu.VMEM(mesh_state.shape, bf16),
        in_specs=[hbm] * 16,
        out_specs=pl.BlockSpec(memory_space=pltpu.VMEM),
        scratch_shapes=scratch,
        compiler_params=pltpu.CompilerParams(
            collective_id=0, has_side_effects=True, vmem_limit_bytes=60 * 1024 * 1024
        ),
    )(
        mesh_state,
        boundary,
        grid_edges.T,
        mesh_edges.T,
        jnp.transpose(boundary_send, SEND_ORDER),
        boundary_count,
        edge_tiles,
        halo_source,
        halo_count,
        edge_first,
        edge_second,
        node_first,
        node_second,
        edge_bias,
        node_bias,
        node_gain,
    )


def solution(mesh):
    in_specs = (
        P(("groups", "member"), ("space", "chan"), None, None),
        P(("groups", "member"), "space", None, None),
        P("groups", None, None),
        P("groups", None),
        P(("groups", "space", "chan"), None),
        P(("groups", "space")),
        P(("groups", "space")),
        P(("groups", "space")),
        P(("groups", "space", "chan"), None),
        P(),
        P(),
        P(),
        P(),
        P(),
        P(),
        P(),
    )
    out_specs = P(("groups", "member"), ("space", "chan"), None, None)
    return jax.shard_map(
        functools.partial(body, mesh.shape["space"]),
        mesh=mesh,
        in_specs=in_specs,
        out_specs=out_specs,
        check_vma=False,
    )
```

```python
import functools

import jax
import jax.numpy as jnp
from jax import lax
from jax.experimental import pallas as pl
from jax.experimental.pallas import tpu as pltpu
from jax.sharding import PartitionSpec as P

MESH = pl.DeviceIdType.MESH
ROWS = 32
UNROLL = 4
SEND_ORDER = (2, 0, 1)


def dot(left, right):
    return jnp.dot(left, right, preferred_element_type=jnp.float32)


def kernel(
    n,
    mesh_state,
    boundary,
    grid_edges,
    mesh_edges,
    boundary_send_in,
    boundary_count_in,
    edge_tiles_in,
    halo_source_in,
    halo_count_in,
    edge_first,
    edge_second,
    node_first,
    node_second,
    edge_bias_in,
    node_bias_in,
    node_gain_in,
    out,
    boundary_send,
    boundary_count,
    edge_tiles,
    halo_source,
    halo_count,
    edge_bias,
    node_bias,
    node_gain,
    bound,
    picked,
    slots,
    targets,
    encoded,
    edge_out,
    edge_in,
    result,
    first,
    second,
    node_a,
    node_b,
    source_proj,
    target_proj,
    hidden,
    own_grid,
    own_mesh,
    far_grid,
    far_mesh,
    grid_index,
    mesh_index,
    halo_table,
    local_sem,
    state_sem,
    state_send,
    state_recv,
    index_send,
    index_recv,
    slot_send,
    slot_recv,
    halo_send,
    halo_recv,
    out_local,
    out_send,
    out_recv,
):
    space, chan = lax.axis_index("space"), lax.axis_index("chan")
    other = 1 - chan
    half = bound.shape[1]
    chunks = half // ROWS
    tiles_own = mesh_state.shape[1]
    tiles = 2 * tiles_own
    cap = boundary_send.shape[0]
    edges = edge_tiles.shape[0]
    halo = halo_source.shape[0]
    zero_tile = source_proj.shape[0] - 1
    features = targets.shape[2]

    def start_row(side, chunk):
        return pl.multiple_of(side * half + chunk * ROWS, ROWS)

    barrier = pltpu.get_barrier_semaphore()
    for step in range(1, n):
        pl.semaphore_signal(
            barrier, inc=1, device_id={"space": lax.rem(space + step, n)}, device_id_type=MESH
        )
    pl.semaphore_signal(barrier, inc=1, device_id={"chan": other}, device_id_type=MESH)

    get_bound = pltpu.make_async_copy(
        boundary.at[0, :, pl.ds(start_row(chan, 0), half), :], bound, local_sem.at[0]
    )
    get_bound.start()
    table_copies = [
        pltpu.make_async_copy(boundary_send_in, boundary_send, local_sem.at[7]),
        pltpu.make_async_copy(boundary_count_in, boundary_count, local_sem.at[8]),
    ]
    for copy in table_copies:
        copy.start()
    index_copies = [
        pltpu.make_async_copy(edge_tiles_in, edge_tiles, local_sem.at[9]),
        pltpu.make_async_copy(halo_source_in, halo_source, local_sem.at[10]),
        pltpu.make_async_copy(halo_count_in, halo_count, local_sem.at[11]),
        pltpu.make_async_copy(grid_edges, own_grid, local_sem.at[1]),
        pltpu.make_async_copy(mesh_edges, own_mesh, local_sem.at[2]),
    ]
    weight_copies = [
        pltpu.make_async_copy(edge_bias_in, edge_bias, local_sem.at[12]),
        pltpu.make_async_copy(node_bias_in, node_bias, local_sem.at[13]),
        pltpu.make_async_copy(node_gain_in, node_gain, local_sem.at[14]),
        pltpu.make_async_copy(edge_first, first, local_sem.at[3]),
        pltpu.make_async_copy(edge_second, second, local_sem.at[4]),
        pltpu.make_async_copy(node_first, node_a, local_sem.at[5]),
        pltpu.make_async_copy(node_second, node_b, local_sem.at[6]),
    ]
    state_local = pltpu.make_async_copy(
        mesh_state.at[0, :, pl.ds(start_row(chan, 0), half), :],
        targets.at[pl.ds(chan * tiles_own, tiles_own)],
        state_sem,
    )
    state_local.start()
    for copy in index_copies + weight_copies:
        copy.start()

    get_bound.wait()
    for copy in table_copies:
        copy.wait()

    def pick(partition, chunk):
        values = []
        for c in range(cap):
            tile = bound[boundary_send[c, space, partition], pl.ds(chunk * ROWS, ROWS), :]
            live = jnp.where(c < boundary_count[space, partition], 1.0, 0.0)
            values.append((tile.astype(jnp.float32) * live).astype(jnp.bfloat16))
        return values

    sends = []
    slot_copies = []
    for chunk in range(chunks):
        for step in range(1, n):
            for c, value in enumerate(pick(lax.rem(space + step, n), chunk)):
                picked[chunk, step - 1, c] = value
        if chunk == 0:
            pl.semaphore_wait(barrier, n)
        row = []
        for step in range(1, n):
            copy = pltpu.make_async_remote_copy(
                src_ref=picked.at[chunk, step - 1],
                dst_ref=slots.at[chunk, space],
                send_sem=slot_send.at[chunk, step - 1],
                recv_sem=slot_recv.at[chunk, step - 1],
                device_id={"space": lax.rem(space + step, n)},
                device_id_type=MESH,
            )
            copy.start()
            row.append(copy)
        slot_copies.append(row)
        sends += row

    far_index = []
    for number, (source, target) in enumerate(((grid_edges, far_grid), (mesh_edges, far_mesh))):
        copy = pltpu.make_async_remote_copy(
            src_ref=source,
            dst_ref=target,
            send_sem=index_send.at[number],
            recv_sem=index_recv.at[number],
            device_id={"chan": other},
            device_id_type=MESH,
        )
        copy.start()
        far_index.append(copy)
    sends += far_index
    state_copies = []
    for chunk in range(chunks):
        copy = pltpu.make_async_remote_copy(
            src_ref=mesh_state.at[0, :, pl.ds(start_row(other, chunk), ROWS), :],
            dst_ref=targets.at[pl.ds(chan * tiles_own, tiles_own), pl.ds(chunk * ROWS, ROWS), :],
            send_sem=state_send.at[chunk],
            recv_sem=state_recv.at[chunk],
            device_id={"chan": other},
            device_id_type=MESH,
        )
        copy.start()
        state_copies.append(copy)
    sends += state_copies

    for chunk in range(chunks):
        for c, value in enumerate(pick(space, chunk)):
            slots[chunk, space, c] = value
    for copy in index_copies:
        copy.wait()
    for tile in range(tiles):
        halo_table[tile] = tile
    for h in range(halo):
        halo_table[tiles + h] = jnp.where(
            h < halo_count[0], tiles + halo_source[h], zero_tile
        )
    source_proj[zero_tile] = jnp.zeros((ROWS, features), jnp.float32)
    for copy in far_index:
        copy.wait_recv()

    def index_step(tile, carry):
        near, far = chan * tiles_own + tile, other * tiles_own + tile
        for k in range(grid_index.shape[1]):
            grid_index[near, k] = own_grid[k, tile]
            grid_index[far, k] = far_grid[k, tile]
        for k in range(mesh_index.shape[1]):
            mesh_index[near, k] = halo_table[own_mesh[k, tile]]
            mesh_index[far, k] = halo_table[far_mesh[k, tile]]
        return carry

    lax.fori_loop(0, tiles_own, index_step, 0)
    for copy in weight_copies:
        copy.wait()
    state_local.wait()

    def project_target(layer, target):
        target_proj[...] = (
            (dot(target, first[layer, 1]) + edge_bias[layer : layer + 1, :]) * 0.5
        ).reshape(target_proj.shape)

    def interact(layer, target, index):

        def tile_step(tile, carry):
            base = target_proj[tile]
            total = None
            for k in range(index.shape[1]):
                value = source_proj[index[tile, k]] + base
                term = value * jnp.tanh(value) + value
                total = term if total is None else total + term
            hidden[tile] = total.astype(jnp.bfloat16)
            return carry

        lax.fori_loop(0, tiles, tile_step, 0, unroll=UNROLL)
        sums = hidden[...].reshape(tiles * ROWS, features)
        aggregate = dot(sums, second[layer]).astype(jnp.bfloat16)
        value = 0.5 * (
            dot(target, node_a[layer, 0])
            + dot(aggregate, node_a[layer, 1])
            + node_bias[layer : layer + 1, :]
        )
        inner = (value * jnp.tanh(value) + value).astype(jnp.bfloat16)
        node_sum = dot(inner, node_b[layer])
        center = node_sum - jnp.mean(node_sum, axis=-1, keepdims=True)
        spread = jnp.mean(center * center, axis=-1, keepdims=True)
        normed = center * lax.rsqrt(spread + 1e-05) * node_gain[layer : layer + 1, :]
        return (target.astype(jnp.float32) + normed).astype(jnp.bfloat16)

    def project(tiles_in, layer, begin):
        count = tiles_in.shape[0] // ROWS
        source_proj[begin : begin + count] = (dot(tiles_in, first[layer, 0]) * 0.5).reshape(
            count, ROWS, features
        )

    halo_copies = []

    def encode(chunk):
        rows = pl.ds(chunk * ROWS, ROWS)
        state_copies[chunk].wait_recv()
        target = targets[:, rows, :].reshape(tiles * ROWS, features)
        project_target(0, target)
        for copy in slot_copies[chunk]:
            copy.wait_recv()
        project(slots[chunk].reshape(n * cap * ROWS, features), 0, 0)
        encoded[:, rows, :] = interact(0, target, grid_index).reshape(tiles, ROWS, features)
        for j in range(edges):
            value = encoded[edge_tiles[j], rows, :]
            edge_out[chunk, j] = value
            edge_in[chunk, space, j] = value
        row = []
        for step in range(1, n):
            copy = pltpu.make_async_remote_copy(
                src_ref=edge_out.at[chunk],
                dst_ref=edge_in.at[chunk, space],
                send_sem=halo_send.at[chunk, step - 1],
                recv_sem=halo_recv.at[chunk, step - 1],
                device_id={"space": lax.rem(space + step, n)},
                device_id_type=MESH,
            )
            copy.start()
            row.append(copy)
        halo_copies.append(row)

    local_outs, far_outs = [], []

    def process(chunk):
        rows = pl.ds(chunk * ROWS, ROWS)
        target = encoded[:, rows, :].reshape(tiles * ROWS, features)
        project(target, 1, 0)
        project_target(1, target)
        for copy in halo_copies[chunk]:
            copy.wait_recv()
        project(edge_in[chunk].reshape(n * edges * ROWS, features), 1, tiles)
        result[:, rows, :] = interact(1, target, mesh_index).reshape(tiles, ROWS, features)
        place = out.at[0, :, pl.ds(start_row(chan, chunk), ROWS), :]
        far = pltpu.make_async_remote_copy(
            src_ref=result.at[pl.ds(other * tiles_own, tiles_own), rows, :],
            dst_ref=place,
            send_sem=out_send.at[chunk],
            recv_sem=out_recv.at[chunk],
            device_id={"chan": other},
            device_id_type=MESH,
        )
        far.start()
        far_outs.append(far)
        near = pltpu.make_async_copy(
            result.at[pl.ds(chan * tiles_own, tiles_own), rows, :], place, out_local.at[chunk]
        )
        near.start()
        local_outs.append(near)

    for chunk in range(chunks):
        encode(chunk)
    for chunk in range(chunks):
        process(chunk)

    for copy in sends:
        copy.wait_send()
    for row in halo_copies:
        for copy in row:
            copy.wait_send()
    for copy in local_outs + far_outs:
        copy.wait()


def body(
    n,
    mesh_state,
    boundary,
    boundary_send,
    boundary_count,
    grid_edges,
    edge_tiles,
    halo_source,
    halo_count,
    mesh_edges,
    edge_first,
    edge_bias,
    edge_second,
    node_first,
    node_bias,
    node_second,
    node_gain,
):
    _, own, tile, features = mesh_state.shape
    half = tile // 2
    chunks = half // ROWS
    tiles = 2 * own
    cap = boundary_send.shape[2]
    edges = edge_tiles.shape[0]
    halo = halo_source.shape[0]
    count = max(n * cap, tiles + n * edges) + 1
    bf16, f32, i32 = jnp.bfloat16, jnp.float32, jnp.int32
    dma = pltpu.SemaphoreType.DMA
    scratch = [
        pltpu.SMEM(tuple(boundary_send.shape[axis] for axis in SEND_ORDER), i32),
        pltpu.SMEM(boundary_count.shape, i32),
        pltpu.SMEM(edge_tiles.shape, i32),
        pltpu.SMEM(halo_source.shape, i32),
        pltpu.SMEM(halo_count.shape, i32),
        pltpu.VMEM(edge_bias.shape, f32),
        pltpu.VMEM(node_bias.shape, f32),
        pltpu.VMEM(node_gain.shape, f32),
        pltpu.VMEM((boundary.shape[1], half, features), bf16),
        pltpu.VMEM((chunks, n - 1, cap, ROWS, features), bf16),
        pltpu.VMEM((chunks, n, cap, ROWS, features), bf16),
        pltpu.VMEM((tiles, half, features), bf16),
        pltpu.VMEM((tiles, half, features), bf16),
        pltpu.VMEM((chunks, edges, ROWS, features), bf16),
        pltpu.VMEM((chunks, n, edges, ROWS, features), bf16),
        pltpu.VMEM((tiles, half, features), bf16),
        pltpu.VMEM(edge_first.shape, bf16),
        pltpu.VMEM(edge_second.shape, bf16),
        pltpu.VMEM(node_first.shape, bf16),
        pltpu.VMEM(node_second.shape, bf16),
        pltpu.VMEM((count, ROWS, features), f32),
        pltpu.VMEM((tiles, ROWS, features), f32),
        pltpu.VMEM((tiles, ROWS, features), bf16),
        pltpu.SMEM(grid_edges.shape[::-1], i32),
        pltpu.SMEM(mesh_edges.shape[::-1], i32),
        pltpu.SMEM(grid_edges.shape[::-1], i32),
        pltpu.SMEM(mesh_edges.shape[::-1], i32),
        pltpu.SMEM((tiles, grid_edges.shape[1]), i32),
        pltpu.SMEM((tiles, mesh_edges.shape[1]), i32),
        pltpu.SMEM((tiles + halo,), i32),
        dma((15,)),
        dma,
        dma((chunks,)),
        dma((chunks,)),
        dma((2,)),
        dma((2,)),
        dma((chunks, n - 1)),
        dma((chunks, n - 1)),
        dma((chunks, n - 1)),
        dma((chunks, n - 1)),
        dma((chunks,)),
        dma((chunks,)),
        dma((chunks,)),
    ]
    hbm = pl.BlockSpec(memory_space=pltpu.HBM)
    return pl.pallas_call(
        functools.partial(kernel, n),
        out_shape=pltpu.VMEM(mesh_state.shape, bf16),
        in_specs=[hbm] * 16,
        out_specs=pl.BlockSpec(memory_space=pltpu.VMEM),
        scratch_shapes=scratch,
        compiler_params=pltpu.CompilerParams(
            collective_id=0, has_side_effects=True, vmem_limit_bytes=60 * 1024 * 1024
        ),
    )(
        mesh_state,
        boundary,
        grid_edges.T,
        mesh_edges.T,
        jnp.transpose(boundary_send, SEND_ORDER),
        boundary_count,
        edge_tiles,
        halo_source,
        halo_count,
        edge_first,
        edge_second,
        node_first,
        node_second,
        edge_bias,
        node_bias,
        node_gain,
    )


def solution(mesh):
    in_specs = (
        P(("groups", "member"), ("space", "chan"), None, None),
        P(("groups", "member"), "space", None, None),
        P("groups", None, None),
        P("groups", None),
        P(("groups", "space", "chan"), None),
        P(("groups", "space")),
        P(("groups", "space")),
        P(("groups", "space")),
        P(("groups", "space", "chan"), None),
        P(),
        P(),
        P(),
        P(),
        P(),
        P(),
        P(),
    )
    out_specs = P(("groups", "member"), ("space", "chan"), None, None)
    return jax.shard_map(
        functools.partial(body, mesh.shape["space"]),
        mesh=mesh,
        in_specs=in_specs,
        out_specs=out_specs,
        check_vma=False,
    )
```
